512 devices in a mesh: dp: 8 (over z), ctx: 16 (over y, x_lo), head: 4 (over x_hi, core).
Axes of the slice: x: 4 (x_hi: 2, x_lo: 2; x = x_hi * 2 + x_lo), y: 8, z: 8, core: 2. Of those that a mesh axis runs over, the one named last changes fastest.
Arguments:
- queries: bfloat16 [8, 2048, 64, 128], P('dp', 'ctx', 'head'), may hold values from -4.5 to 4.5
- keys: bfloat16 [8, 2048, 8, 128], P('dp', 'ctx', 'head'), may hold values from -4.5 to 4.5
- values: bfloat16 [8, 2048, 8, 128], P('dp', 'ctx', 'head'), may hold values from -6 to 6
- map_query: bfloat16 [64, 128, 64], P('head'), may hold values from -1.390625 to 1.390625
- map_key: bfloat16 [64, 128, 64], P('head'), may hold values from -1.390625 to 1.390625
Outputs:
- grad_query_map: float32 [64, 128, 64], P('head')
- grad_key_map: float32 [64, 128, 64], P('head')
- head_loss: float32 [64], P('head')
The draws below stay inside these ranges and needn't reach their ends.
All inputs are finite; a program needn't handle non-finite values.
Results may differ from the reference program's by a relative error of at most 0.0038.
Values may be sent and summed in bfloat16 or wider, within the bound.
No kernel may reach another device: no remote copies, remote signals or barrier semaphores. Data moves between devices by JAX's collectives and lax.ppermute only.
A program may use at most 128 MiB of HBM per device.

```python
from functools import partial
import jax
import jax.numpy as jnp
from jax import lax

HEADS = 64
KV = 8
DH = 128
FEAT = 64
TOK_DEV = 128
BATCH = 8
LENGTH = 2048


def draw_queries(key, part):
    key = jax.random.fold_in(key, 11)
    full_shape = (BATCH, LENGTH, HEADS, DH)
    drawn = jnp.clip(jax.random.normal(key, full_shape, jnp.float32), -4.5, 4.5)
    return drawn.astype(jnp.bfloat16)


def draw_keys(key, part):
    key = jax.random.fold_in(key, 13)
    full_shape = (BATCH, LENGTH, KV, DH)
    drawn = jnp.clip(jax.random.normal(key, full_shape, jnp.float32), -4.5, 4.5)
    return drawn.astype(jnp.bfloat16)


def mapping_draw(key):
    full_shape = (HEADS, DH, FEAT)
    drawn = jnp.clip(jax.random.normal(key, full_shape, jnp.float32), -4.5, 4.5) * DH ** (-0.5)
    return drawn.astype(jnp.bfloat16)


def draw_map_query(key, part):
    key = jax.random.fold_in(key, 17)
    return mapping_draw(key)


def draw_map_key(key, part):
    key = jax.random.fold_in(key, 19)
    return mapping_draw(key)


def shard_levels(own_key, shape, cuts, smallest, top_value):
    level, own = 1.0, jax.random.fold_in(own_key, 6)
    for dim, blocks in cuts:
        draws = jnp.exp(jax.random.uniform(jax.random.fold_in(own, dim), (blocks,), jnp.float32, smallest / len(cuts), top_value / len(cuts)))
        level = level * jnp.repeat(draws, shape[dim] // blocks).reshape([-1 if axis == dim else 1 for axis in range(len(shape))])
    return level


def gaussian(rng, extent, scale, reach, pieces=(), held_as=jnp.bfloat16):
    gain = shard_levels(rng, extent, pieces, -0.22, 0.18) if pieces else 1.0
    result = jax.random.normal(rng, extent, jnp.float32) * scale * gain
    return jnp.minimum(jnp.maximum(result, -reach), reach).astype(held_as)


def setup_inputs(seed: int = 0) -> dict:
    streams_of = jax.random.split(jax.random.key(seed), 6)
    queries = draw_queries(jax.random.fold_in(streams_of[5], 71), 0)
    keys = draw_keys(jax.random.fold_in(streams_of[5], 71), 0)
    values = gaussian(streams_of[2], (BATCH, LENGTH, KV, DH), 1.0, 6.0, ((0, 8), (1, 16), (2, 4)))
    map_query = draw_map_query(jax.random.fold_in(streams_of[5], 71), 0)
    map_key = draw_map_key(jax.random.fold_in(streams_of[5], 71), 0)
    return dict(queries=queries, keys=keys, values=values, map_query=map_query, map_key=map_key)


HIGH = lax.Precision.HIGHEST


def product(pattern, left_side, right_side):
    return jnp.einsum(pattern, left_side.astype(jnp.float32), right_side.astype(jnp.float32), precision=HIGH)


def features(inputs, mapping):
    logits = product("thd,hdf->thf", inputs, mapping)
    positive = jax.nn.softmax(logits, axis=-1)
    negative = jax.nn.softmax(-logits, axis=-1)
    joined = jnp.concatenate([positive, negative], -1).astype(jnp.bfloat16)
    return joined, positive, negative


def lower_mask(length_rows):
    positions = jnp.arange(length_rows)
    return positions[:, None] >= positions[None, :]


def block_forward(query_features, key_features, values_block, carried, totals):
    causal = lower_mask(query_features.shape[0])
    scores = jnp.where(causal[None], product("thf,shf->hts", query_features, key_features), 0.0)
    numerator = product("hts,shd->thd", scores, values_block) + product("thf,hfd->thd", query_features, carried)
    denominator = jnp.transpose(jnp.sum(scores, -1)) + product("thf,hf->th", query_features, totals)
    return numerator / denominator[..., None], denominator


def block_backward(query_features, key_features, values_block, gradient_numerator, gradient_denominator, carried, totals, suffix_state, suffix_totals):
    causal = lower_mask(query_features.shape[0])
    weights = product("thd,shd->hts", gradient_numerator, values_block) + jnp.transpose(gradient_denominator)[:, :, None]
    weights = jnp.where(causal[None], weights, 0.0)
    query_gradient = product("hts,shf->thf", weights, key_features) + product("hfd,thd->thf", carried, gradient_numerator) + gradient_denominator[:, :, None] * totals[None]
    key_gradient = product("hts,thf->shf", weights, query_features) + product("hfd,shd->shf", suffix_state, values_block) + suffix_totals[None]
    return query_gradient, key_gradient


def map_gradient(inputs, positive, negative, feature_gradient):
    half_width = positive.shape[-1]
    positive_gradient = feature_gradient[..., :half_width]
    negative_gradient = feature_gradient[..., half_width:]
    logit_gradient = positive * (positive_gradient - jnp.sum(positive_gradient * positive, -1, keepdims=True))
    logit_gradient = logit_gradient - negative * (negative_gradient - jnp.sum(negative_gradient * negative, -1, keepdims=True))
    return product("thd,thf->hdf", inputs, logit_gradient)


def teacher_sequence(sequence_queries, sequence_keys, sequence_values, group_size):
    causal = lower_mask(sequence_queries.shape[0])

    def one_head(head_index):
        query_head = lax.dynamic_index_in_dim(sequence_queries, head_index, 1, False)
        key_head = lax.dynamic_index_in_dim(sequence_keys, head_index // group_size, 1, False)
        value_head = lax.dynamic_index_in_dim(sequence_values, head_index // group_size, 1, False)
        scores = jnp.dot(query_head, key_head.T, preferred_element_type=jnp.float32) * (DH ** -0.5)
        scores = jnp.where(causal, scores, -jnp.inf)
        row_peak = jnp.max(scores, -1, keepdims=True)
        expo = jnp.exp(scores - row_peak)
        mass_sum = jnp.sum(expo, -1, keepdims=True)
        return jnp.dot(expo.astype(jnp.bfloat16), value_head, preferred_element_type=jnp.float32) / mass_sum

    head_outputs = lax.map(one_head, jnp.arange(HEADS).astype(jnp.int32))
    return jnp.transpose(head_outputs, (1, 0, 2))


def reference(queries, keys, values, map_query, map_key):
    group_size = HEADS // KV
    blocks = LENGTH // TOK_DEV
    token_count = BATCH * LENGTH

    def cut(tensor):
        return tensor.reshape((blocks, TOK_DEV) + tensor.shape[1:])

    def exclusive(tensor):
        return jnp.concatenate([jnp.zeros_like(tensor[:1]), jnp.cumsum(tensor, 0)[:-1]], 0)

    def one_sequence(sequence_index):
        sequence_queries = lax.dynamic_index_in_dim(queries, sequence_index, 0, False)
        sequence_keys = lax.dynamic_index_in_dim(keys, sequence_index, 0, False)
        sequence_values = lax.dynamic_index_in_dim(values, sequence_index, 0, False)
        target = teacher_sequence(sequence_queries, sequence_keys, sequence_values, group_size)
        wide_keys = jnp.repeat(sequence_keys, group_size, axis=1)
        wide_values = jnp.repeat(sequence_values, group_size, axis=1)
        query_features, query_positive, query_negative = features(sequence_queries, map_query)
        key_features, key_positive, key_negative = features(wide_keys, map_key)
        block_states = jax.vmap(partial(product, "shf,shd->hfd"))(cut(key_features), cut(wide_values))
        block_totals = jnp.sum(cut(key_features).astype(jnp.float32), 1)
        carried = exclusive(block_states)
        totals = exclusive(block_totals)
        student, denominator = jax.vmap(block_forward)(cut(query_features), cut(key_features), cut(wide_values), carried, totals)
        residual = student - cut(target)
        head_loss = jnp.sum(residual * residual, (0, 1, 3)) / token_count
        student_gradient = 2.0 * residual / token_count
        gradient_numerator = student_gradient / denominator[..., None]
        gradient_denominator = -jnp.sum(student_gradient * student, -1) / denominator
        block_later = jax.vmap(partial(product, "thf,thd->hfd"))(cut(query_features), gradient_numerator)
        block_later_totals = jax.vmap(partial(product, "thf,th->hf"))(cut(query_features), gradient_denominator)
        suffix_state = jnp.flip(exclusive(jnp.flip(block_later, 0)), 0)
        suffix_totals = jnp.flip(exclusive(jnp.flip(block_later_totals, 0)), 0)
        query_gradient, key_gradient = jax.vmap(block_backward)(cut(query_features), cut(key_features), cut(wide_values), gradient_numerator, gradient_denominator, carried, totals, suffix_state, suffix_totals)
        query_map_gradient = jnp.sum(jax.vmap(map_gradient)(cut(sequence_queries), cut(query_positive), cut(query_negative), query_gradient), 0)
        key_map_gradient = jnp.sum(jax.vmap(map_gradient)(cut(wide_keys), cut(key_positive), cut(key_negative), key_gradient), 0)
        return query_map_gradient, key_map_gradient, head_loss

    query_parts, key_parts, loss_parts = lax.map(one_sequence, jnp.arange(BATCH).astype(jnp.int32))
    return jnp.sum(query_parts, 0), jnp.sum(key_parts, 0), jnp.sum(loss_parts, 0)
```

```python
import functools
import math

import jax
import jax.numpy as jnp
from jax import lax
from jax.experimental import pallas as pl
from jax.experimental.pallas import tpu as pltpu
from jax.sharding import PartitionSpec as P

F32 = jnp.float32
BF16 = jnp.bfloat16
CHUNK = 256
LOSS_ROWS = 16


def nn(left, right):
    return lax.dot_general(left, right, (((1,), (0,)), ((), ())), preferred_element_type=F32)


def nt(left, right):
    return lax.dot_general(left, right, (((1,), (1,)), ((), ())), preferred_element_type=F32)


def halves(array):
    high = array.astype(BF16)
    return high, (array - high.astype(F32)).astype(BF16)


def wide_nn(left, right):
    rows = left.shape[0]
    both = nn(jnp.concatenate(halves(left), 0), right)
    return both[:rows] + both[rows:]


def sort_rows(groups):
    rows = 256
    span = rows // groups
    to = lax.broadcasted_iota(jnp.int32, (rows, rows), 0)
    source = lax.broadcasted_iota(jnp.int32, (rows, rows), 1)
    wanted = lax.rem(to, span) * groups + lax.div(to, span)
    return (source == wanted).astype(F32).astype(BF16)


def pack_kernel(q_ref, k_ref, v_ref, out_ref):
    heads = out_ref.shape[0]
    tokens = out_ref.shape[1] // 3
    value_heads = k_ref.shape[0] // tokens
    group = heads // value_heads
    span = 256 // heads
    order = sort_rows(heads)
    for step in range(tokens // span):
        rows = nn(order, q_ref[step * 256 : (step + 1) * 256, :]).astype(BF16)
        out_ref[:, step * span : (step + 1) * span, :] = rows.reshape(heads, span, rows.shape[-1])
    order = sort_rows(value_heads)
    span = 256 // value_heads
    for place, ref in ((tokens, k_ref), (2 * tokens, v_ref)):
        for step in range(tokens // span):
            rows = nn(order, ref[step * 256 : (step + 1) * 256, :]).astype(BF16)
            start = place + step * span
            for head in range(heads):
                own = head // group
                out_ref[head, start : start + span, :] = rows[own * span : (own + 1) * span, :]


def feature_halves(inputs, mapping_t):
    logits = nt(mapping_t, inputs)
    positive = jnp.exp(logits - jnp.max(logits, 0, keepdims=True))
    negative = jnp.exp(jnp.min(logits, 0, keepdims=True) - logits)
    positive = positive / jnp.sum(positive, 0, keepdims=True)
    negative = negative / jnp.sum(negative, 0, keepdims=True)
    return positive, negative


def logit_gradient(positive, negative, gradient):
    half = positive.shape[0]
    up = gradient[:half]
    down = gradient[half:]
    up = positive * (up - jnp.sum(up * positive, 0, keepdims=True))
    down = negative * (down - jnp.sum(down * negative, 0, keepdims=True))
    return up - down


def head_kernel(token_count, x_ref, mq_ref, mk_ref, out_ref, kp, kn, qf, w_ref, g_ref):
    blocks, rows3, size = x_ref.shape
    tokens = rows3 // 3
    per = CHUNK // tokens
    chunks = blocks // per
    feat = mq_ref.shape[-1]
    scale = size**-0.5 * math.log2(math.e)
    mq_t = mq_ref[...].astype(F32).T.astype(BF16)
    mk_t = mk_ref[...].astype(F32).T.astype(BF16)

    def part(which, first, last):
        piece = x_ref[first * per : last * per, which * tokens : (which + 1) * tokens, :]
        return piece.reshape((last - first) * CHUNK, size)

    row = lax.broadcasted_iota(jnp.int32, (CHUNK, CHUNK), 0)
    col = lax.broadcasted_iota(jnp.int32, (CHUNK, CHUNK), 1)
    causal = row >= col
    state = jnp.zeros((2 * feat, 2 * size), F32)
    query_map = jnp.zeros((feat, size), F32)
    loss = jnp.zeros((CHUNK, size), F32)
    for c in range(chunks):
        q = part(0, c, c + 1)
        k = part(1, c, c + 1)
        v = part(2, c, c + 1)
        last = jnp.where(causal, nt(q, k), -jnp.inf)
        peak = jnp.max(last, -1, keepdims=True)
        if c:
            first = nt(q, part(1, 0, c))
            peak = jnp.maximum(peak, jnp.max(first, -1, keepdims=True))
        expo = jnp.exp2((last - peak) * scale)
        mass = jnp.sum(expo, -1, keepdims=True)
        target = nn(expo.astype(BF16), v)
        if c:
            expo = jnp.exp2((first - peak) * scale)
            mass = mass + jnp.sum(expo, -1, keepdims=True)
            target = target + nn(expo.astype(BF16), part(2, 0, c))
        target = target / mass
        q_up, q_down = feature_halves(q, mq_t)
        k_up, k_down = feature_halves(k, mk_t)
        kp[c] = k_up
        kn[c] = k_down
        q_joined = jnp.concatenate([q_up, q_down], 0)
        phi_qt = q_joined.astype(BF16)
        phi_q = q_joined.T.astype(BF16)
        phi_kt = jnp.concatenate([k_up, k_down], 0).astype(BF16)
        qf[c] = phi_qt
        v_wide = jnp.concatenate([v, jnp.ones_like(v)], 1)
        scores = jnp.where(causal, nn(phi_q, phi_kt), 0.0)
        score_high, score_low = halves(scores)
        state_low = state.astype(BF16)
        summed = nn(score_high, v_wide) + nn(score_low, v_wide) + nn(phi_q, state_low)
        inverse = 1.0 / summed[:, size:]
        student = summed[:, :size] * inverse
        residual = student - target
        loss = loss + residual * residual
        gradient = residual * inverse * (2.0 / token_count)
        wide = jnp.concatenate([gradient, -gradient * student], 1).astype(BF16)
        g_ref[c] = wide
        weights = jnp.where(causal, nt(wide, v_wide), 0.0).astype(BF16)
        w_ref[c] = weights
        q_gradient = nt(phi_kt, weights) + nt(state_low, wide)
        state = state + nn(phi_kt, v_wide)
        query_map = query_map + wide_nn(logit_gradient(q_up, q_down, q_gradient), q)
    suffix = jnp.zeros((2 * feat, 2 * size), F32)
    key_map = jnp.zeros((feat, size), F32)
    for c in reversed(range(chunks)):
        k = part(1, c, c + 1)
        v = part(2, c, c + 1)
        v_wide = jnp.concatenate([v, jnp.ones_like(v)], 1)
        phi_qt = qf[c]
        k_gradient = nn(phi_qt, w_ref[c]) + nt(suffix.astype(BF16), v_wide)
        suffix = suffix + nn(phi_qt, g_ref[c])
        key_map = key_map + wide_nn(logit_gradient(kp[c], kn[c], k_gradient), k)
    maps = jnp.concatenate([query_map, key_map], 0).T
    out_ref[0:size, :] = maps.astype(BF16)
    total = jnp.sum(jnp.sum(loss, 0, keepdims=True), 1, keepdims=True) * (1.0 / token_count)
    out_ref[size:, :] = loss_rows(total)


def loss_rows(total):
    high = jnp.broadcast_to(total, (LOSS_ROWS, 128)).astype(BF16).astype(F32)
    low = total - high
    row = lax.broadcasted_iota(jnp.int32, (LOSS_ROWS, 128), 0)
    return jnp.where(row == 0, high, jnp.where(row == 1, low, 0.0)).astype(BF16)


def add_kernel(x_ref, out_ref):
    size = x_ref.shape[1] - LOSS_ROWS
    total = x_ref[0].astype(F32)
    for place in range(1, x_ref.shape[0]):
        total = total + x_ref[place].astype(F32)
    maps = total[:size].astype(BF16)
    loss = loss_rows(total[size : size + 1, 0:1] + total[size + 1 : size + 2, 0:1])
    for place in range(out_ref.shape[0]):
        out_ref[place, 0:size, :] = maps
        out_ref[place, size:, :] = loss


def spread_kernel(x_ref, query_ref, key_ref, loss_ref):
    size = query_ref.shape[1]
    feat = query_ref.shape[2]
    for head in range(x_ref.shape[0]):
        maps = x_ref[head, 0:size, :].astype(F32)
        query_ref[head] = maps[:, :feat]
        key_ref[head] = maps[:, feat:]
        tail = x_ref[head, size:, :].astype(F32)
        loss_ref[head : head + 1, :] = tail[0:1, :] + tail[1:2, :]


VMEM = pl.BlockSpec(memory_space=pltpu.VMEM)


def call(kernel, shapes, inputs, scratch=(), limit=32):
    many = isinstance(shapes, (list, tuple))
    return pl.pallas_call(
        kernel,
        out_shape=shapes,
        in_specs=[VMEM] * len(inputs),
        out_specs=[VMEM] * len(shapes) if many else VMEM,
        scratch_shapes=list(scratch),
        compiler_params=pltpu.CompilerParams(vmem_limit_bytes=limit * 2**20),
    )(*inputs)


def shards(queries, keys, values, map_query, map_key):
    _, tokens, heads, size = queries.shape
    feat = map_query.shape[-1]
    dp = lax.axis_size("dp")
    ctx = lax.axis_size("ctx")
    token_count = dp * ctx * tokens
    shape = jax.ShapeDtypeStruct
    packed = call(
        pack_kernel,
        shape((heads, 3 * tokens, size), BF16),
        [queries.reshape(-1, size), keys.reshape(-1, size), values.reshape(-1, size)],
    )
    mine = lax.axis_index("ctx")
    own_query = lax.dynamic_index_in_dim(map_query, mine, 0, False)
    own_key = lax.dynamic_index_in_dim(map_key, mine, 0, False)
    sequence = lax.all_to_all(packed, "ctx", 0, 0, tiled=True)
    chunks = ctx * tokens // CHUNK
    part = call(
        functools.partial(head_kernel, token_count),
        shape((size + LOSS_ROWS, size), BF16),
        [sequence, own_query, own_key],
        [
            pltpu.VMEM((chunks, feat, CHUNK), F32),
            pltpu.VMEM((chunks, feat, CHUNK), F32),
            pltpu.VMEM((chunks, 2 * feat, CHUNK), BF16),
            pltpu.VMEM((chunks, CHUNK, CHUNK), BF16),
            pltpu.VMEM((chunks, CHUNK, 2 * size), BF16),
        ],
        48,
    )
    parts = jnp.broadcast_to(part[None], (dp,) + part.shape)
    parts = lax.all_to_all(parts, "dp", 0, 0, tiled=True)
    whole = call(add_kernel, shape((ctx,) + part.shape, BF16), [parts])
    gathered = lax.all_to_all(whole, "ctx", 0, 0, tiled=True)
    grad_query, grad_key, loss = call(
        spread_kernel,
        [shape((heads, size, feat), F32), shape((heads, size, feat), F32), shape((heads, size), F32)],
        [gathered],
    )
    return grad_query, grad_key, loss[:, 0]


def solution(mesh):
    placed = P("dp", "ctx", "head", None)
    maps = P("head", None, None)
    return jax.shard_map(
        shards,
        mesh=mesh,
        in_specs=(placed, placed, placed, maps, maps),
        out_specs=(maps, maps, P("head")),
        check_vma=False,
    )
```

```python
import functools
import math

import jax
import jax.numpy as jnp
from jax import lax
from jax.experimental import pallas as pl
from jax.experimental.pallas import tpu as pltpu
from jax.sharding import PartitionSpec as P

F32 = jnp.float32
BF16 = jnp.bfloat16
CHUNK = 256
LOSS_ROWS = 16


def nn(left, right):
    return lax.dot_general(left, right, (((1,), (0,)), ((), ())), preferred_element_type=F32)


def nt(left, right):
    return lax.dot_general(left, right, (((1,), (1,)), ((), ())), preferred_element_type=F32)


def halves(array):
    high = array.astype(BF16)
    return high, (array - high.astype(F32)).astype(BF16)


def wide_nn(left, right):
    rows = left.shape[0]
    both = nn(jnp.concatenate(halves(left), 0), right)
    return both[:rows] + both[rows:]


def sort_rows(groups):
    rows = 256
    span = rows // groups
    shift = span.bit_length() - 1
    to = lax.broadcasted_iota(jnp.int32, (rows, rows), 0)
    source = lax.broadcasted_iota(jnp.int32, (rows, rows), 1)
    wanted = (to & (span - 1)) * groups + (to >> shift)
    return (source == wanted).astype(F32).astype(BF16)


def pack_kernel(q_hbm, k_hbm, v_hbm, out_ref, q_ref, k_ref, v_ref, sems):
    copies = [
        pltpu.make_async_copy(source, target, sems.at[place])
        for place, (source, target) in enumerate(((k_hbm, k_ref), (v_hbm, v_ref), (q_hbm, q_ref)))
    ]
    for copy in copies:
        copy.start()
    heads = out_ref.shape[0]
    tokens = out_ref.shape[1] // 3
    value_heads = k_ref.shape[0] // tokens
    group = heads // value_heads
    order = sort_rows(heads)
    value_order = sort_rows(value_heads)
    for place, ref in enumerate((k_ref, v_ref)):
        span = 256 // value_heads
        copies[place].wait()
        for step in range(tokens // span):
            rows = nn(value_order, ref[step * 256 : (step + 1) * 256, :]).astype(BF16)
            start = (place + 1) * tokens + step * span
            for head in range(heads):
                own = head // group
                out_ref[head, start : start + span, :] = rows[own * span : (own + 1) * span, :]
    span = 256 // heads
    copies[2].wait()
    for step in range(tokens // span):
        rows = nn(order, q_ref[step * 256 : (step + 1) * 256, :]).astype(BF16)
        out_ref[:, step * span : (step + 1) * span, :] = rows.reshape(heads, span, rows.shape[-1])


def feature_halves(inputs, mapping_t):
    logits = nt(mapping_t, inputs)
    positive = jnp.exp(logits - jnp.max(logits, 0, keepdims=True))
    negative = jnp.exp(jnp.min(logits, 0, keepdims=True) - logits)
    positive = positive / jnp.sum(positive, 0, keepdims=True)
    negative = negative / jnp.sum(negative, 0, keepdims=True)
    return positive, negative


def logit_gradient(positive, negative, gradient):
    half = positive.shape[0]
    up = gradient[:half]
    down = gradient[half:]
    up = positive * (up - jnp.sum(up * positive, 0, keepdims=True))
    down = negative * (down - jnp.sum(down * negative, 0, keepdims=True))
    return up - down


def head_kernel(token_count, x_ref, mq_ref, mk_ref, out_ref):
    blocks, rows3, size = x_ref.shape
    tokens = rows3 // 3
    per = CHUNK // tokens
    chunks = range(blocks // per)
    feat = mq_ref.shape[0]
    scale = size**-0.5 * math.log2(math.e)

    def part(which, first, last):
        piece = x_ref[first * per : last * per, which * tokens : (which + 1) * tokens, :]
        return piece.reshape((last - first) * CHUNK, size)

    def each(make):
        return [make(c) for c in chunks]

    row = lax.broadcasted_iota(jnp.int32, (CHUNK, CHUNK), 0)
    col = lax.broadcasted_iota(jnp.int32, (CHUNK, CHUNK), 1)
    causal = row >= col
    q = each(lambda c: part(0, c, c + 1))
    k = each(lambda c: part(1, c, c + 1))
    ones = jnp.ones((CHUNK, size), BF16)
    v_wide = each(lambda c: jnp.concatenate([part(2, c, c + 1), ones], 1))
    mq_t = mq_ref[...]
    mk_t = mk_ref[...]

    k_up, k_down = zip(*each(lambda c: feature_halves(k[c], mk_t)))
    q_up, q_down = zip(*each(lambda c: feature_halves(q[c], mq_t)))
    phi_kt = each(lambda c: jnp.concatenate([k_up[c], k_down[c]], 0).astype(BF16))
    q_joined = each(lambda c: jnp.concatenate([q_up[c], q_down[c]], 0))
    phi_qt = each(lambda c: q_joined[c].astype(BF16))
    phi_q = each(lambda c: q_joined[c].T.astype(BF16))
    state = [jnp.zeros((2 * feat, 2 * size), F32)]
    for c in chunks[:-1]:
        state.append(state[-1] + nn(phi_kt[c], v_wide[c]))
    state_low = each(lambda c: state[c].astype(BF16))
    scores = each(lambda c: halves(jnp.where(causal, nn(phi_q[c], phi_kt[c]), 0.0)))

    def teacher(c):
        last = jnp.where(causal, nt(q[c], k[c]), -jnp.inf)
        peak = jnp.max(last, -1, keepdims=True)
        if c:
            first = nt(q[c], part(1, 0, c))
            peak = jnp.maximum(peak, jnp.max(first, -1, keepdims=True))
        expo = jnp.exp2((last - peak) * scale)
        mass = jnp.sum(expo, -1, keepdims=True)
        target = nn(expo.astype(BF16), part(2, c, c + 1))
        if c:
            expo = jnp.exp2((first - peak) * scale)
            mass = mass + jnp.sum(expo, -1, keepdims=True)
            target = target + nn(expo.astype(BF16), part(2, 0, c))
        return target / mass

    target = each(teacher)
    summed = each(
        lambda c: nn(scores[c][0], v_wide[c]) + nn(scores[c][1], v_wide[c]) + nn(phi_q[c], state_low[c])
    )
    loss = jnp.zeros((CHUNK, size), F32)
    wide = []
    for c in chunks:
        inverse = 1.0 / summed[c][:, size:]
        student = summed[c][:, :size] * inverse
        residual = student - target[c]
        loss = loss + residual * residual
        gradient = residual * inverse * (2.0 / token_count)
        wide.append(jnp.concatenate([gradient, -gradient * student], 1).astype(BF16))
    suffix = [jnp.zeros((2 * feat, 2 * size), F32)]
    for c in reversed(chunks[1:]):
        suffix.insert(0, suffix[0] + nn(phi_qt[c], wide[c]))
    weights = each(lambda c: halves(jnp.where(causal, nt(wide[c], v_wide[c]), 0.0)))
    q_gradient = each(
        lambda c: nt(phi_kt[c], weights[c][0]) + nt(phi_kt[c], weights[c][1]) + nt(state_low[c], wide[c])
    )
    k_gradient = each(
        lambda c: nn(phi_qt[c], weights[c][0])
        + nn(phi_qt[c], weights[c][1])
        + nt(suffix[c].astype(BF16), v_wide[c])
    )
    query_map = sum(each(lambda c: wide_nn(logit_gradient(q_up[c], q_down[c], q_gradient[c]), q[c])))
    key_map = sum(each(lambda c: wide_nn(logit_gradient(k_up[c], k_down[c], k_gradient[c]), k[c])))
    maps = jnp.concatenate([query_map, key_map], 0)
    out_ref[0:size, :] = maps.astype(BF16)
    total = jnp.sum(jnp.sum(loss, 0, keepdims=True), 1, keepdims=True) * (1.0 / token_count)
    out_ref[size:, :] = loss_rows(total)


def loss_rows(total):
    high = jnp.broadcast_to(total, (LOSS_ROWS, 128)).astype(BF16).astype(F32)
    low = total - high
    row = lax.broadcasted_iota(jnp.int32, (LOSS_ROWS, 128), 0)
    return jnp.where(row == 0, high, jnp.where(row == 1, low, 0.0)).astype(BF16)


def add_kernel(x_ref, out_ref):
    size = x_ref.shape[1] - LOSS_ROWS
    total = x_ref[0].astype(F32)
    for place in range(1, x_ref.shape[0]):
        total = total + x_ref[place].astype(F32)
    maps = total[:size].astype(BF16)
    loss = loss_rows(total[size : size + 1, 0:1] + total[size + 1 : size + 2, 0:1])
    for place in range(out_ref.shape[0]):
        out_ref[place, 0:size, :] = maps
        out_ref[place, size:, :] = loss


def spread_kernel(x_ref, query_hbm, key_hbm, loss_ref, query_ref, key_ref, sems):
    heads, feat, _ = query_ref.shape
    size = 2 * feat
    parts = sems.shape[1]
    each = heads // parts
    lane = lax.broadcasted_iota(jnp.int32, (1, heads), 1)
    loss = jnp.zeros((1, heads), F32)
    copies = []
    for part in range(parts):
        own = pl.ds(part * each, each)
        for head in range(part * each, (part + 1) * each):
            query_ref[head] = x_ref[head, 0:feat, :].astype(F32)
            key_ref[head] = x_ref[head, feat:size, :].astype(F32)
        for place, (source, target) in enumerate(((query_ref, query_hbm), (key_ref, key_hbm))):
            copies.append(pltpu.make_async_copy(source.at[own], target.at[own], sems.at[place, part]))
            copies[-1].start()
    for head in range(heads):
        tail = x_ref[head, size:, :].astype(F32)
        loss = jnp.where(lane == head, tail[0:1, :heads] + tail[1:2, :heads], loss)
    loss_ref[...] = loss
    for copy in copies:
        copy.wait()


VMEM = pl.BlockSpec(memory_space=pltpu.VMEM)


HBM = pl.BlockSpec(memory_space=pltpu.HBM)


def call(kernel, shapes, inputs, scratch=(), limit=32, in_specs=None, out_specs=VMEM):
    return pl.pallas_call(
        kernel,
        out_shape=shapes,
        in_specs=in_specs or [VMEM] * len(inputs),
        out_specs=out_specs,
        scratch_shapes=list(scratch),
        compiler_params=pltpu.CompilerParams(vmem_limit_bytes=limit * 2**20),
    )(*inputs)


def head_call(sequence, own_query, own_key, token_count):
    blocks, rows, size = sequence.shape
    chunks = blocks * rows // 3 // CHUNK
    return call(
        functools.partial(head_kernel, token_count),
        jax.ShapeDtypeStruct((size + LOSS_ROWS, size), BF16),
        [sequence, own_query, own_key],
        (),
        48,
    )


def shards(queries, keys, values, map_query, map_key):
    _, tokens, heads, size = queries.shape
    feat = map_query.shape[-1]
    dp = lax.axis_size("dp")
    ctx = lax.axis_size("ctx")
    token_count = dp * ctx * tokens
    shape = jax.ShapeDtypeStruct
    rows = [
        pltpu.with_memory_space_constraint(array.reshape(-1, size), pltpu.HBM)
        for array in (queries, keys, values)
    ]
    packed = call(
        pack_kernel,
        shape((heads, 3 * tokens, size), BF16),
        rows,
        [pltpu.VMEM(array.shape, BF16) for array in rows] + [pltpu.SemaphoreType.DMA((3,))],
        in_specs=[HBM] * 3,
    )
    mine = lax.axis_index("ctx")
    own_query = lax.dynamic_index_in_dim(jnp.swapaxes(map_query, 1, 2), mine, 0, False)
    own_key = lax.dynamic_index_in_dim(jnp.swapaxes(map_key, 1, 2), mine, 0, False)
    sequence = lax.all_to_all(packed, "ctx", 0, 0, tiled=True)
    part = head_call(sequence, own_query, own_key, token_count)
    parts = jnp.broadcast_to(part[None], (dp,) + part.shape)
    parts = lax.all_to_all(parts, "dp", 0, 0, tiled=True)
    whole = call(add_kernel, shape((ctx,) + part.shape, BF16), [parts])
    gathered = lax.all_to_all(whole, "ctx", 0, 0, tiled=True)
    maps = (heads, feat, size)
    grad_query, grad_key, loss = call(
        spread_kernel,
        [shape(maps, F32), shape(maps, F32), shape((1, heads), F32)],
        [gathered],
        [pltpu.VMEM(maps, F32), pltpu.VMEM(maps, F32), pltpu.SemaphoreType.DMA((2, 2))],
        out_specs=[HBM, HBM, VMEM],
    )
    return jnp.swapaxes(grad_query, 1, 2), jnp.swapaxes(grad_key, 1, 2), loss.reshape(heads)


def solution(mesh):
    placed = P("dp", "ctx", "head", None)
    maps = P("head", None, None)
    return jax.shard_map(
        shards,
        mesh=mesh,
        in_specs=(placed, placed, placed, maps, maps),
        out_specs=(maps, maps, P("head")),
        check_vma=False,
    )
```

```python
import functools
import math

import jax
import jax.numpy as jnp
from jax import lax
from jax.experimental import pallas as pl
from jax.experimental.pallas import tpu as pltpu
from jax.sharding import PartitionSpec as P

F32 = jnp.float32
BF16 = jnp.bfloat16
CHUNK = 256
LOSS_ROWS = 8


def nn(left, right):
    return lax.dot_general(left, right, (((1,), (0,)), ((), ())), preferred_element_type=F32)


def nt(left, right):
    return lax.dot_general(left, right, (((1,), (1,)), ((), ())), preferred_element_type=F32)


def halves(array):
    high = array.astype(BF16)
    return high, (array - high.astype(F32)).astype(BF16)


def wide_nn(left, right):
    rows = left.shape[0]
    both = nn(jnp.concatenate(halves(left), 0), right)
    return both[:rows] + both[rows:]


def sort_rows(groups):
    rows = 256
    span = rows // groups
    shift = span.bit_length() - 1
    to = lax.broadcasted_iota(jnp.int32, (rows, rows), 0)
    source = lax.broadcasted_iota(jnp.int32, (rows, rows), 1)
    wanted = (to & (span - 1)) * groups + (to >> shift)
    return (source == wanted).astype(F32).astype(BF16)


def pack_kernel(q_hbm, k_hbm, v_hbm, out_ref, q_ref, k_ref, v_ref, sems):
    copies = [
        pltpu.make_async_copy(source, target, sems.at[place])
        for place, (source, target) in enumerate(((k_hbm, k_ref), (v_hbm, v_ref), (q_hbm, q_ref)))
    ]
    for copy in copies:
        copy.start()
    heads = out_ref.shape[0]
    tokens = out_ref.shape[1] // 3
    value_heads = k_ref.shape[0] // tokens
    group = heads // value_heads
    order = sort_rows(heads)
    value_order = sort_rows(value_heads)
    for place, ref in enumerate((k_ref, v_ref)):
        span = 256 // value_heads
        copies[place].wait()
        for step in range(tokens // span):
            rows = nn(value_order, ref[step * 256 : (step + 1) * 256, :]).astype(BF16)
            start = (place + 1) * tokens + step * span
            for head in range(heads):
                own = head // group
                out_ref[head, start : start + span, :] = rows[own * span : (own + 1) * span, :]
    span = 256 // heads
    copies[2].wait()
    for step in range(tokens // span):
        rows = nn(order, q_ref[step * 256 : (step + 1) * 256, :]).astype(BF16)
        out_ref[:, step * span : (step + 1) * span, :] = rows.reshape(heads, span, rows.shape[-1])


def feature_halves(inputs, mapping_t):
    logits = nt(mapping_t, inputs)
    positive = jnp.exp(logits - jnp.max(logits, 0, keepdims=True))
    negative = jnp.exp(jnp.min(logits, 0, keepdims=True) - logits)
    positive = positive / jnp.sum(positive, 0, keepdims=True)
    negative = negative / jnp.sum(negative, 0, keepdims=True)
    return positive, negative


def logit_gradient(positive, negative, gradient):
    half = positive.shape[0]
    up = gradient[:half]
    down = gradient[half:]
    up = positive * (up - jnp.sum(up * positive, 0, keepdims=True))
    down = negative * (down - jnp.sum(down * negative, 0, keepdims=True))
    return up - down


def head_kernel(token_count, x_ref, mq_ref, mk_ref, out_ref):
    blocks, rows3, size = x_ref.shape
    tokens = rows3 // 3
    per = CHUNK // tokens
    chunks = range(blocks // per)
    feat = mq_ref.shape[0]
    scale = size**-0.5 * math.log2(math.e)

    def part(which, first, last):
        piece = x_ref[first * per : last * per, which * tokens : (which + 1) * tokens, :]
        return piece.reshape((last - first) * CHUNK, size)

    def each(make):
        return [make(c) for c in chunks]

    row = lax.broadcasted_iota(jnp.int32, (CHUNK, CHUNK), 0)
    col = lax.broadcasted_iota(jnp.int32, (CHUNK, CHUNK), 1)
    causal = row >= col
    q = each(lambda c: part(0, c, c + 1))
    k = each(lambda c: part(1, c, c + 1))
    ones = jnp.ones((CHUNK, size), BF16)
    v_wide = each(lambda c: jnp.concatenate([part(2, c, c + 1), ones], 1))
    mq_t = mq_ref[...]
    mk_t = mk_ref[...]

    def feature(c):
        k_halves = feature_halves(k[c], mk_t)
        q_halves = feature_halves(q[c], mq_t)
        q_joined = jnp.concatenate(q_halves, 0)
        phi_kt = jnp.concatenate(k_halves, 0).astype(BF16)
        return k_halves, q_halves, phi_kt, q_joined.astype(BF16), q_joined.T.astype(BF16)

    def block(c):
        last = jnp.where(causal, nt(q[c], k[c]), -jnp.inf)
        if not c:
            return (last,)
        return nt(q[c], part(1, 0, c)), last

    def peak(c):
        return functools.reduce(jnp.maximum, [jnp.max(s, -1, keepdims=True) for s in blocks_of[c]])

    def teacher(c):
        expos = [jnp.exp2((s - peaks[c]) * scale) for s in blocks_of[c]]
        mass = sum(jnp.sum(e, -1, keepdims=True) for e in expos)
        target = nn(expos[-1].astype(BF16), part(2, c, c + 1))
        if c:
            target = target + nn(expos[0].astype(BF16), part(2, 0, c))
        return target / mass

    def score(c):
        return halves(jnp.where(causal, nn(phi_q[c], phi_kt[c]), 0.0))

    blocks_of = each(block)
    peaks = each(peak)
    made, target = zip(*each(lambda c: (feature(c), teacher(c))))
    k_halves, q_halves, phi_kt, phi_qt, phi_q = zip(*made)
    k_up, k_down = zip(*k_halves)
    q_up, q_down = zip(*q_halves)
    state = [jnp.zeros((2 * feat, 2 * size), F32)]
    for c in chunks[:-1]:
        state.append(state[-1] + nn(phi_kt[c], v_wide[c]))
    state_low = each(lambda c: state[c].astype(BF16))
    scores = each(score)
    summed = each(
        lambda c: nn(scores[c][0], v_wide[c]) + nn(scores[c][1], v_wide[c]) + nn(phi_q[c], state_low[c])
    )
    loss = jnp.zeros((CHUNK, size), F32)
    wide = []
    for c in chunks:
        inverse = 1.0 / summed[c][:, size:]
        student = summed[c][:, :size] * inverse
        residual = student - target[c]
        loss = loss + residual * residual
        gradient = residual * inverse * (2.0 / token_count)
        wide.append(jnp.concatenate([gradient, -gradient * student], 1).astype(BF16))
    suffix = [jnp.zeros((2 * feat, 2 * size), F32)]
    for c in reversed(chunks[1:]):
        suffix.insert(0, suffix[0] + nn(phi_qt[c], wide[c]))
    weights = each(lambda c: halves(jnp.where(causal, nt(wide[c], v_wide[c]), 0.0)))
    q_gradient = each(
        lambda c: nt(phi_kt[c], weights[c][0]) + nt(phi_kt[c], weights[c][1]) + nt(state_low[c], wide[c])
    )
    k_gradient = each(
        lambda c: nn(phi_qt[c], weights[c][0])
        + nn(phi_qt[c], weights[c][1])
        + nt(suffix[c].astype(BF16), v_wide[c])
    )
    query_map = sum(each(lambda c: wide_nn(logit_gradient(q_up[c], q_down[c], q_gradient[c]), q[c])))
    key_map = sum(each(lambda c: wide_nn(logit_gradient(k_up[c], k_down[c], k_gradient[c]), k[c])))
    maps = jnp.concatenate([query_map, key_map], 0)
    out_ref[0:size, :] = maps.astype(BF16)
    total = jnp.sum(jnp.sum(loss, 0, keepdims=True), 1, keepdims=True) * (1.0 / token_count)
    out_ref[size:, :] = loss_rows(total)


def loss_rows(total):
    high = jnp.broadcast_to(total, (LOSS_ROWS, 128)).astype(BF16).astype(F32)
    low = total - high
    row = lax.broadcasted_iota(jnp.int32, (LOSS_ROWS, 128), 0)
    return jnp.where(row == 0, high, jnp.where(row == 1, low, 0.0)).astype(BF16)


def add_kernel(x_ref, out_ref):
    size = x_ref.shape[1] - LOSS_ROWS
    total = x_ref[0].astype(F32)
    for place in range(1, x_ref.shape[0]):
        total = total + x_ref[place].astype(F32)
    maps = total[:size].astype(BF16)
    loss = loss_rows(total[size : size + 1, 0:1] + total[size + 1 : size + 2, 0:1])
    for place in range(out_ref.shape[0]):
        out_ref[place, 0:size, :] = maps
        out_ref[place, size:, :] = loss


def spread_kernel(x_ref, query_hbm, key_hbm, loss_ref, query_ref, key_ref, sems):
    heads, feat, _ = query_ref.shape
    size = 2 * feat
    parts = sems.shape[1]
    each = heads // parts
    lane = lax.broadcasted_iota(jnp.int32, (1, heads), 1)
    loss = jnp.zeros((1, heads), F32)
    copies = []
    for part in range(parts):
        own = pl.ds(part * each, each)
        for head in range(part * each, (part + 1) * each):
            query_ref[head] = x_ref[head, 0:feat, :].astype(F32)
            key_ref[head] = x_ref[head, feat:size, :].astype(F32)
        for place, (source, target) in enumerate(((query_ref, query_hbm), (key_ref, key_hbm))):
            copies.append(pltpu.make_async_copy(source.at[own], target.at[own], sems.at[place, part]))
            copies[-1].start()
    for head in range(heads):
        tail = x_ref[head, size:, :].astype(F32)
        loss = jnp.where(lane == head, tail[0:1, :heads] + tail[1:2, :heads], loss)
    loss_ref[...] = loss
    for copy in copies:
        copy.wait()


VMEM = pl.BlockSpec(memory_space=pltpu.VMEM)


HBM = pl.BlockSpec(memory_space=pltpu.HBM)


def call(kernel, shapes, inputs, scratch=(), limit=32, in_specs=None, out_specs=VMEM):
    return pl.pallas_call(
        kernel,
        out_shape=shapes,
        in_specs=in_specs or [VMEM] * len(inputs),
        out_specs=out_specs,
        scratch_shapes=list(scratch),
        compiler_params=pltpu.CompilerParams(vmem_limit_bytes=limit * 2**20),
    )(*inputs)


def head_call(sequence, own_query, own_key, token_count):
    blocks, rows, size = sequence.shape
    chunks = blocks * rows // 3 // CHUNK
    return call(
        functools.partial(head_kernel, token_count),
        jax.ShapeDtypeStruct((size + LOSS_ROWS, size), BF16),
        [sequence, own_query, own_key],
        (),
        48,
    )


def pack_call(queries, keys, values):
    _, tokens, heads, size = queries.shape
    rows = [
        pltpu.with_memory_space_constraint(array.reshape(-1, size), pltpu.HBM)
        for array in (queries, keys, values)
    ]
    return call(
        pack_kernel,
        jax.ShapeDtypeStruct((heads, 3 * tokens, size), BF16),
        rows,
        [pltpu.VMEM(array.shape, BF16) for array in rows] + [pltpu.SemaphoreType.DMA((3,))],
        in_specs=[HBM] * 3,
    )


def spread_call(gathered, feat):
    heads, rows, size = gathered.shape
    maps = (heads, feat, size)
    shape = jax.ShapeDtypeStruct
    return call(
        spread_kernel,
        [shape(maps, F32), shape(maps, F32), shape((1, heads), F32)],
        [gathered],
        [pltpu.VMEM(maps, F32), pltpu.VMEM(maps, F32), pltpu.SemaphoreType.DMA((2, 2))],
        out_specs=[HBM, HBM, VMEM],
    )


def shards(queries, keys, values, map_query, map_key):
    _, tokens, heads, size = queries.shape
    feat = map_query.shape[-1]
    dp = lax.axis_size("dp")
    ctx = lax.axis_size("ctx")
    token_count = dp * ctx * tokens
    shape = jax.ShapeDtypeStruct
    packed = pack_call(queries, keys, values)
    mine = lax.axis_index("ctx")
    own_query = lax.dynamic_index_in_dim(jnp.swapaxes(map_query, 1, 2), mine, 0, False)
    own_key = lax.dynamic_index_in_dim(jnp.swapaxes(map_key, 1, 2), mine, 0, False)
    sequence = lax.all_to_all(packed, "ctx", 0, 0, tiled=True)
    part = head_call(sequence, own_query, own_key, token_count)
    parts = jnp.broadcast_to(part[None], (dp,) + part.shape)
    parts = lax.all_to_all(parts, "dp", 0, 0, tiled=True)
    whole = call(add_kernel, shape((ctx,) + part.shape, BF16), [parts])
    gathered = lax.all_to_all(whole, "ctx", 0, 0, tiled=True)
    grad_query, grad_key, loss = spread_call(gathered, feat)
    return jnp.swapaxes(grad_query, 1, 2), jnp.swapaxes(grad_key, 1, 2), loss.reshape(heads)


def solution(mesh):
    placed = P("dp", "ctx", "head", None)
    maps = P("head", None, None)
    return jax.shard_map(
        shards,
        mesh=mesh,
        in_specs=(placed, placed, placed, maps, maps),
        out_specs=(maps, maps, P("head")),
        check_vma=False,
    )
```

```python
import functools
import math

import jax
import jax.numpy as jnp
from jax import lax
from jax.experimental import pallas as pl
from jax.experimental.pallas import tpu as pltpu
from jax.sharding import PartitionSpec as P

F32 = jnp.float32
BF16 = jnp.bfloat16
CHUNK = 256
EXCHANGE = [0, 14, 2, 12, 4, 10, 6, 8, 1, 15, 3, 13, 5, 11, 7, 9]
GATHER = [10, 5, 0, 1, 9, 4, 6, 2, 3, 15, 11, 7, 12, 8, 13, 14]


def nn(left, right):
    return lax.dot_general(left, right, (((1,), (0,)), ((), ())), preferred_element_type=F32)


def nt(left, right):
    return lax.dot_general(left, right, (((1,), (1,)), ((), ())), preferred_element_type=F32)


def halves(array):
    high = array.astype(BF16)
    return high, (array - high.astype(F32)).astype(BF16)


def wide_nn(left, right):
    rows = left.shape[0]
    both = nn(jnp.concatenate(halves(left), 0), right)
    return both[:rows] + both[rows:]


def sort_rows(groups):
    rows = 256
    span = rows // groups
    shift = span.bit_length() - 1
    to = lax.broadcasted_iota(jnp.int32, (rows, rows), 0)
    source = lax.broadcasted_iota(jnp.int32, (rows, rows), 1)
    wanted = (to & (span - 1)) * groups + (to >> shift)
    return (source == wanted).astype(F32).astype(BF16)


def pack_kernel(q_hbm, k_hbm, v_hbm, out_ref, q_ref, k_ref, v_ref, sems):
    copies = [
        pltpu.make_async_copy(source, target, sems.at[place])
        for place, (source, target) in enumerate(((k_hbm, k_ref), (v_hbm, v_ref), (q_hbm, q_ref)))
    ]
    for copy in copies:
        copy.start()
    heads = out_ref.shape[0]
    tokens = out_ref.shape[1] // 3
    value_heads = k_ref.shape[0] // tokens
    group = heads // value_heads
    order = sort_rows(heads)
    value_order = sort_rows(value_heads)
    for place, ref in enumerate((k_ref, v_ref)):
        span = 256 // value_heads
        copies[place].wait()
        for step in range(tokens // span):
            rows = nn(value_order, ref[step * 256 : (step + 1) * 256, :]).astype(BF16)
            start = (place + 1) * tokens + step * span
            for head in range(heads):
                own = head // group
                out_ref[head, start : start + span, :] = rows[own * span : (own + 1) * span, :]
    span = 256 // heads
    copies[2].wait()
    for step in range(tokens // span):
        rows = nn(order, q_ref[step * 256 : (step + 1) * 256, :]).astype(BF16)
        out_ref[:, step * span : (step + 1) * span, :] = rows.reshape(heads, span, rows.shape[-1])


def feature_halves(inputs, mapping_t):
    logits = nt(mapping_t, inputs)
    positive = jnp.exp(logits - jnp.max(logits, 0, keepdims=True))
    negative = jnp.exp(jnp.min(logits, 0, keepdims=True) - logits)
    positive = positive * (1.0 / jnp.sum(positive, 0, keepdims=True))
    negative = negative * (1.0 / jnp.sum(negative, 0, keepdims=True))
    return positive, negative


def logit_gradient(positive, negative, gradient):
    half = positive.shape[0]
    up = gradient[:half]
    down = gradient[half:]
    up = positive * (up - jnp.sum(up * positive, 0, keepdims=True))
    down = negative * (down - jnp.sum(down * negative, 0, keepdims=True))
    return up - down


def head_kernel(token_count, x_ref, mq_ref, mk_ref, out_ref):
    blocks, rows3, size = x_ref.shape
    tokens = rows3 // 3
    per = CHUNK // tokens
    chunks = range(blocks // per)
    feat = mq_ref.shape[0]
    scale = size**-0.5 * math.log2(math.e)

    def part(which, first, last):
        slots = [EXCHANGE.index(block) for block in range(first * per, last * per)]
        rows = slice(which * tokens, (which + 1) * tokens)
        return jnp.concatenate([x_ref[slot, rows, :] for slot in slots], 0)

    def each(make):
        return [make(c) for c in chunks]

    row = lax.broadcasted_iota(jnp.int32, (CHUNK, CHUNK), 0)
    col = lax.broadcasted_iota(jnp.int32, (CHUNK, CHUNK), 1)
    causal = row >= col
    q = each(lambda c: part(0, c, c + 1))
    k = each(lambda c: part(1, c, c + 1))
    ones = jnp.ones((CHUNK, size), BF16)
    v_wide = each(lambda c: jnp.concatenate([part(2, c, c + 1), ones], 1))
    mq_t = mq_ref[...]
    mk_t = mk_ref[...]

    def feature(c):
        k_halves = feature_halves(k[c], mk_t)
        q_halves = feature_halves(q[c], mq_t)
        q_joined = jnp.concatenate(q_halves, 0)
        phi_kt = jnp.concatenate(k_halves, 0).astype(BF16)
        return k_halves, q_halves, phi_kt, q_joined.astype(BF16), q_joined.T.astype(BF16)

    def block(c):
        last = jnp.where(causal, nt(q[c], k[c]), -jnp.inf)
        if not c:
            return (last,)
        return nt(q[c], part(1, 0, c)), last

    def peak(c):
        return functools.reduce(jnp.maximum, [jnp.max(s, -1, keepdims=True) for s in blocks_of[c]])

    def teacher(c):
        expos = [jnp.exp2((s - peaks[c]) * scale) for s in blocks_of[c]]
        mass = sum(jnp.sum(e, -1, keepdims=True) for e in expos)
        target = nn(expos[-1].astype(BF16), part(2, c, c + 1))
        if c:
            target = target + nn(expos[0].astype(BF16), part(2, 0, c))
        return target * (1.0 / mass)

    def score(c):
        return halves(jnp.where(causal, nn(phi_q[c], phi_kt[c]), 0.0))

    blocks_of = each(block)
    peaks = each(peak)
    target, made = zip(*each(lambda c: (teacher(c), feature(c))))
    k_halves, q_halves, phi_kt, phi_qt, phi_q = zip(*made)
    k_up, k_down = zip(*k_halves)
    q_up, q_down = zip(*q_halves)
    state = [jnp.zeros((2 * feat, 2 * size), F32)]
    for c in chunks[:-1]:
        state.append(state[-1] + nn(phi_kt[c], v_wide[c]))
    state_low = each(lambda c: state[c].astype(BF16))
    scores = each(score)
    summed = each(
        lambda c: nn(scores[c][0], v_wide[c]) + nn(scores[c][1], v_wide[c]) + nn(phi_q[c], state_low[c])
    )
    loss = jnp.zeros((CHUNK, size), F32)
    wide = []
    for c in chunks:
        inverse = 1.0 / summed[c][:, size:]
        student = summed[c][:, :size] * inverse
        residual = student - target[c]
        loss = loss + residual * residual
        gradient = residual * inverse * (2.0 / token_count)
        wide.append(jnp.concatenate([gradient, -gradient * student], 1).astype(BF16))
    suffix = [jnp.zeros((2 * feat, 2 * size), F32)]
    for c in reversed(chunks[1:]):
        suffix.insert(0, suffix[0] + nn(phi_qt[c], wide[c]))
    weights = each(lambda c: halves(jnp.where(causal, nt(wide[c], v_wide[c]), 0.0)))
    q_gradient = each(
        lambda c: nt(phi_kt[c], weights[c][0]) + nt(phi_kt[c], weights[c][1]) + nt(state_low[c], wide[c])
    )
    k_gradient = each(
        lambda c: nn(phi_qt[c], weights[c][0])
        + nn(phi_qt[c], weights[c][1])
        + nt(suffix[c].astype(BF16), v_wide[c])
    )
    query_map = sum(each(lambda c: wide_nn(logit_gradient(q_up[c], q_down[c], q_gradient[c]), q[c])))
    key_map = sum(each(lambda c: wide_nn(logit_gradient(k_up[c], k_down[c], k_gradient[c]), k[c])))
    total = jnp.sum(jnp.sum(loss, 0, keepdims=True), 1, keepdims=True) * (1.0 / token_count)
    out_ref[...] = with_loss(jnp.concatenate([query_map, key_map], 0), total)


def with_loss(maps, total):
    last = maps.shape[0] // 2 - 1
    high = total.astype(BF16).astype(F32)
    row = lax.broadcasted_iota(jnp.int32, maps.shape, 0)
    col = lax.broadcasted_iota(jnp.int32, maps.shape, 1)
    maps = jnp.where((row == last) & (col == 0), high, maps)
    return jnp.where((row == last) & (col == 1), total - high, maps).astype(BF16)


def add_kernel(x_ref, out_ref):
    total = x_ref[0].astype(F32)
    for place in range(1, x_ref.shape[0]):
        total = total + x_ref[place].astype(F32)
    last = total.shape[0] // 2 - 1
    maps = with_loss(total, total[last : last + 1, 0:1] + total[last : last + 1, 1:2])
    for place in range(out_ref.shape[0]):
        out_ref[place] = maps


def spread_kernel(x_ref, query_hbm, key_hbm, loss_ref, query_ref, key_ref, sems):
    heads, feat, size = query_ref.shape
    row = lax.broadcasted_iota(jnp.int32, (feat, size), 0)
    col = lax.broadcasted_iota(jnp.int32, (feat, size), 1)
    swapped = (row == feat - 1) & (col < 2)
    lane = lax.broadcasted_iota(jnp.int32, (1, heads), 1)
    loss = jnp.zeros((1, heads), F32)
    for head in range(heads):
        slot = GATHER.index(EXCHANGE[head])
        maps = x_ref[slot, 0:feat, :].astype(F32)
        rest = jnp.sum(jnp.where(swapped, 0.0, maps), 0, keepdims=True)
        query_ref[head] = jnp.where(swapped, -rest, maps)
        key_ref[head] = x_ref[slot, feat:, :].astype(F32)
        loss = jnp.where(lane == head, maps[feat - 1 :, 0:1] + maps[feat - 1 :, 1:2], loss)
    loss_ref[...] = loss
    copies = [
        pltpu.make_async_copy(source, target, sems.at[place])
        for place, (source, target) in enumerate(((query_ref, query_hbm), (key_ref, key_hbm)))
    ]
    for copy in copies:
        copy.start()
    for copy in copies:
        copy.wait()


VMEM = pl.BlockSpec(memory_space=pltpu.VMEM)


HBM = pl.BlockSpec(memory_space=pltpu.HBM)


def call(kernel, shapes, inputs, scratch=(), limit=32, in_specs=None, out_specs=VMEM):
    return pl.pallas_call(
        kernel,
        out_shape=shapes,
        in_specs=in_specs or [VMEM] * len(inputs),
        out_specs=out_specs,
        scratch_shapes=list(scratch),
        compiler_params=pltpu.CompilerParams(vmem_limit_bytes=limit * 2**20),
    )(*inputs)


def head_call(sequence, own_query, own_key, token_count):
    blocks, rows, size = sequence.shape
    chunks = blocks * rows // 3 // CHUNK
    return call(
        functools.partial(head_kernel, token_count),
        jax.ShapeDtypeStruct((size, size), BF16),
        [sequence, own_query, own_key],
        (),
        48,
    )


def pack_call(queries, keys, values):
    _, tokens, heads, size = queries.shape
    rows = [
        pltpu.with_memory_space_constraint(array.reshape(-1, size), pltpu.HBM)
        for array in (queries, keys, values)
    ]
    return call(
        pack_kernel,
        jax.ShapeDtypeStruct((heads, 3 * tokens, size), BF16),
        rows,
        [pltpu.VMEM(array.shape, BF16) for array in rows] + [pltpu.SemaphoreType.DMA((3,))],
        in_specs=[HBM] * 3,
    )


def spread_call(gathered, feat):
    heads, rows, size = gathered.shape
    maps = (heads, feat, size)
    shape = jax.ShapeDtypeStruct
    return call(
        spread_kernel,
        [shape(maps, F32), shape(maps, F32), shape((1, heads), F32)],
        [gathered],
        [pltpu.VMEM(maps, F32), pltpu.VMEM(maps, F32), pltpu.SemaphoreType.DMA((2,))],
        out_specs=[HBM, HBM, VMEM],
    )


def shards(queries, keys, values, map_query, map_key):
    _, tokens, heads, size = queries.shape
    feat = map_query.shape[-1]
    dp = lax.axis_size("dp")
    ctx = lax.axis_size("ctx")
    token_count = dp * ctx * tokens
    shape = jax.ShapeDtypeStruct
    packed = pack_call(queries, keys, values)
    places = [EXCHANGE.index(block) for block in range(ctx)]
    mine = jnp.asarray(places, jnp.int32)[lax.axis_index("ctx")]
    own_query = lax.dynamic_index_in_dim(jnp.swapaxes(map_query, 1, 2), mine, 0, False)
    own_key = lax.dynamic_index_in_dim(jnp.swapaxes(map_key, 1, 2), mine, 0, False)
    sequence = lax.all_to_all(packed, "ctx", 0, 0, tiled=True, axis_index_groups=[EXCHANGE])
    part = head_call(sequence, own_query, own_key, token_count)
    parts = jnp.broadcast_to(part[None], (dp,) + part.shape)
    parts = lax.all_to_all(parts, "dp", 0, 0, tiled=True)
    whole = call(add_kernel, shape((ctx,) + part.shape, BF16), [parts])
    gathered = lax.all_to_all(whole, "ctx", 0, 0, tiled=True, axis_index_groups=[GATHER])
    grad_query, grad_key, loss = spread_call(gathered, feat)
    return jnp.swapaxes(grad_query, 1, 2), jnp.swapaxes(grad_key, 1, 2), loss.reshape(heads)


def solution(mesh):
    placed = P("dp", "ctx", "head", None)
    maps = P("head", None, None)
    return jax.shard_map(
        shards,
        mesh=mesh,
        in_specs=(placed, placed, placed, maps, maps),
        out_specs=(maps, maps, P("head")),
        check_vma=False,
    )
```

```python
import functools
import math

import jax
import jax.numpy as jnp
from jax import lax
from jax.experimental import pallas as pl
from jax.experimental.pallas import tpu as pltpu
from jax.sharding import PartitionSpec as P

F32 = jnp.float32
BF16 = jnp.bfloat16
CHUNK = 256
EXCHANGE = [8, 6, 10, 4, 12, 2, 14, 0, 9, 7, 11, 5, 13, 3, 15, 1]
GATHER = [8, 6, 10, 4, 12, 2, 14, 0, 9, 7, 11, 5, 13, 3, 15, 1]
ADD = [6, 3, 0, 5, 7, 1, 4, 2]


def nn(left, right):
    return lax.dot_general(left, right, (((1,), (0,)), ((), ())), preferred_element_type=F32)


def nt(left, right):
    return lax.dot_general(left, right, (((1,), (1,)), ((), ())), preferred_element_type=F32)


def halves(array):
    high = array.astype(BF16)
    return high, (array - high.astype(F32)).astype(BF16)


def wide_nn(left, right):
    rows = left.shape[0]
    both = nn(jnp.concatenate(halves(left), 0), right)
    return both[:rows] + both[rows:]


def sort_rows(groups):
    rows = 256
    span = rows // groups
    shift = span.bit_length() - 1
    to = lax.broadcasted_iota(jnp.int32, (rows, rows), 0)
    source = lax.broadcasted_iota(jnp.int32, (rows, rows), 1)
    wanted = (to & (span - 1)) * groups + (to >> shift)
    return (source == wanted).astype(F32).astype(BF16)


def pack_kernel(q_hbm, k_hbm, v_hbm, out_ref, q_ref, k_ref, v_ref, sems):
    copies = [
        pltpu.make_async_copy(source, target, sems.at[place])
        for place, (source, target) in enumerate(((k_hbm, k_ref), (v_hbm, v_ref), (q_hbm, q_ref)))
    ]
    for copy in copies:
        copy.start()
    heads = out_ref.shape[0]
    tokens = out_ref.shape[1] // 3
    value_heads = k_ref.shape[0] // tokens
    group = heads // value_heads
    order = sort_rows(heads)
    value_order = sort_rows(value_heads)
    for place, ref in enumerate((k_ref, v_ref)):
        span = 256 // value_heads
        copies[place].wait()
        for step in range(tokens // span):
            rows = nn(value_order, ref[step * 256 : (step + 1) * 256, :]).astype(BF16)
            start = (place + 1) * tokens + step * span
            for head in range(heads):
                own = head // group
                out_ref[head, start : start + span, :] = rows[own * span : (own + 1) * span, :]
    span = 256 // heads
    copies[2].wait()
    for step in range(tokens // span):
        rows = nn(order, q_ref[step * 256 : (step + 1) * 256, :]).astype(BF16)
        out_ref[:, step * span : (step + 1) * span, :] = rows.reshape(heads, span, rows.shape[-1])


def feature_halves(inputs, mapping_t):
    logits = nt(mapping_t, inputs)
    positive = jnp.exp(logits - jnp.max(logits, 0, keepdims=True))
    negative = jnp.exp(jnp.min(logits, 0, keepdims=True) - logits)
    positive = positive * (1.0 / jnp.sum(positive, 0, keepdims=True))
    negative = negative * (1.0 / jnp.sum(negative, 0, keepdims=True))
    return positive, negative


def logit_gradient(positive, negative, gradient):
    half = positive.shape[0]
    up = gradient[:half]
    down = gradient[half:]
    up = positive * (up - jnp.sum(up * positive, 0, keepdims=True))
    down = negative * (down - jnp.sum(down * negative, 0, keepdims=True))
    return up - down


def head_kernel(token_count, x_ref, mq_ref, mk_ref, out_ref):
    blocks, rows3, size = x_ref.shape
    tokens = rows3 // 3
    per = CHUNK // tokens
    chunks = range(blocks // per)
    feat = mq_ref.shape[0]
    scale = size**-0.5 * math.log2(math.e)

    def part(which, first, last):
        slots = [EXCHANGE.index(block) for block in range(first * per, last * per)]
        rows = slice(which * tokens, (which + 1) * tokens)
        return jnp.concatenate([x_ref[slot, rows, :] for slot in slots], 0)

    def each(make):
        return [make(c) for c in chunks]

    row = lax.broadcasted_iota(jnp.int32, (CHUNK, CHUNK), 0)
    col = lax.broadcasted_iota(jnp.int32, (CHUNK, CHUNK), 1)
    causal = row >= col
    q = each(lambda c: part(0, c, c + 1))
    k = each(lambda c: part(1, c, c + 1))
    ones = jnp.ones((CHUNK, size), BF16)
    v_wide = each(lambda c: jnp.concatenate([part(2, c, c + 1), ones], 1))
    mq_t = mq_ref[...]
    mk_t = mk_ref[...]

    def feature(c):
        k_halves = feature_halves(k[c], mk_t)
        q_halves = feature_halves(q[c], mq_t)
        q_joined = jnp.concatenate(q_halves, 0)
        phi_kt = jnp.concatenate(k_halves, 0).astype(BF16)
        return k_halves, q_halves, phi_kt, q_joined.astype(BF16), q_joined.T.astype(BF16)

    def block(c):
        last = jnp.where(causal, nt(q[c], k[c]), -jnp.inf)
        if not c:
            return (last,)
        return nt(q[c], part(1, 0, c)), last

    def peak(c):
        return functools.reduce(jnp.maximum, [jnp.max(s, -1, keepdims=True) for s in blocks_of[c]])

    def teacher(c):
        expos = [jnp.exp2((s - peaks[c]) * scale) for s in blocks_of[c]]
        mass = sum(jnp.sum(e, -1, keepdims=True) for e in expos)
        target = nn(expos[-1].astype(BF16), part(2, c, c + 1))
        if c:
            target = target + nn(expos[0].astype(BF16), part(2, 0, c))
        return target * (1.0 / mass)

    def score(c):
        return halves(jnp.where(causal, nn(phi_q[c], phi_kt[c]), 0.0))

    blocks_of = each(block)
    peaks = each(peak)
    target, made = zip(*each(lambda c: (teacher(c), feature(c))))
    k_halves, q_halves, phi_kt, phi_qt, phi_q = zip(*made)
    k_up, k_down = zip(*k_halves)
    q_up, q_down = zip(*q_halves)
    state = [jnp.zeros((2 * feat, 2 * size), F32)]
    for c in chunks[:-1]:
        state.append(state[-1] + nn(phi_kt[c], v_wide[c]))
    state_low = each(lambda c: state[c].astype(BF16))
    scores = each(score)
    summed = each(
        lambda c: nn(scores[c][0], v_wide[c]) + nn(scores[c][1], v_wide[c]) + nn(phi_q[c], state_low[c])
    )
    loss = jnp.zeros((CHUNK, size), F32)
    wide = []
    for c in chunks:
        inverse = 1.0 / summed[c][:, size:]
        student = summed[c][:, :size] * inverse
        residual = student - target[c]
        loss = loss + residual * residual
        gradient = residual * inverse * (2.0 / token_count)
        wide.append(jnp.concatenate([gradient, -gradient * student], 1).astype(BF16))
    suffix = [jnp.zeros((2 * feat, 2 * size), F32)]
    for c in reversed(chunks[1:]):
        suffix.insert(0, suffix[0] + nn(phi_qt[c], wide[c]))
    weights = each(lambda c: halves(jnp.where(causal, nt(wide[c], v_wide[c]), 0.0)))
    q_gradient = each(
        lambda c: nt(phi_kt[c], weights[c][0]) + nt(phi_kt[c], weights[c][1]) + nt(state_low[c], wide[c])
    )
    k_gradient = each(
        lambda c: nn(phi_qt[c], weights[c][0])
        + nn(phi_qt[c], weights[c][1])
        + nt(suffix[c].astype(BF16), v_wide[c])
    )
    query_map = sum(each(lambda c: wide_nn(logit_gradient(q_up[c], q_down[c], q_gradient[c]), q[c])))
    key_map = sum(each(lambda c: wide_nn(logit_gradient(k_up[c], k_down[c], k_gradient[c]), k[c])))
    total = jnp.sum(jnp.sum(loss, 0, keepdims=True), 1, keepdims=True) * (1.0 / token_count)
    out_ref[...] = with_loss(jnp.concatenate([query_map, key_map], 0), total)


def with_loss(maps, total):
    last = maps.shape[0] // 2 - 1
    high = total.astype(BF16).astype(F32)
    row = lax.broadcasted_iota(jnp.int32, maps.shape, 0)
    col = lax.broadcasted_iota(jnp.int32, maps.shape, 1)
    maps = jnp.where((row == last) & (col == 0), high, maps)
    return jnp.where((row == last) & (col == 1), total - high, maps).astype(BF16)


def add_kernel(x_ref, out_ref):
    total = x_ref[0].astype(F32)
    for place in range(1, x_ref.shape[0]):
        total = total + x_ref[place].astype(F32)
    last = total.shape[0] // 2 - 1
    maps = with_loss(total, total[last : last + 1, 0:1] + total[last : last + 1, 1:2])
    for place in range(out_ref.shape[0]):
        out_ref[place] = maps


def spread_kernel(x_ref, query_hbm, key_hbm, loss_ref, query_ref, key_ref, sems):
    heads, feat, size = query_ref.shape
    row = lax.broadcasted_iota(jnp.int32, (feat, size), 0)
    col = lax.broadcasted_iota(jnp.int32, (feat, size), 1)
    swapped = (row == feat - 1) & (col < 2)
    lane = lax.broadcasted_iota(jnp.int32, (1, heads), 1)
    loss = jnp.zeros((1, heads), F32)
    for head in range(heads):
        slot = GATHER.index(EXCHANGE[head])
        maps = x_ref[slot, 0:feat, :].astype(F32)
        rest = jnp.sum(jnp.where(swapped, 0.0, maps), 0, keepdims=True)
        query_ref[head] = jnp.where(swapped, -rest, maps)
        key_ref[head] = x_ref[slot, feat:, :].astype(F32)
        loss = jnp.where(lane == head, maps[feat - 1 :, 0:1] + maps[feat - 1 :, 1:2], loss)
    loss_ref[...] = loss
    copies = [
        pltpu.make_async_copy(source, target, sems.at[place])
        for place, (source, target) in enumerate(((query_ref, query_hbm), (key_ref, key_hbm)))
    ]
    for copy in copies:
        copy.start()
    for copy in copies:
        copy.wait()


VMEM = pl.BlockSpec(memory_space=pltpu.VMEM)


HBM = pl.BlockSpec(memory_space=pltpu.HBM)


def call(kernel, shapes, inputs, scratch=(), limit=32, in_specs=None, out_specs=VMEM):
    return pl.pallas_call(
        kernel,
        out_shape=shapes,
        in_specs=in_specs or [VMEM] * len(inputs),
        out_specs=out_specs,
        scratch_shapes=list(scratch),
        compiler_params=pltpu.CompilerParams(vmem_limit_bytes=limit * 2**20),
    )(*inputs)


def head_call(sequence, own_query, own_key, token_count):
    blocks, rows, size = sequence.shape
    chunks = blocks * rows // 3 // CHUNK
    return call(
        functools.partial(head_kernel, token_count),
        jax.ShapeDtypeStruct((size, size), BF16),
        [sequence, own_query, own_key],
        (),
        48,
    )


def pack_call(queries, keys, values):
    _, tokens, heads, size = queries.shape
    rows = [
        pltpu.with_memory_space_constraint(array.reshape(-1, size), pltpu.HBM)
        for array in (queries, keys, values)
    ]
    return call(
        pack_kernel,
        jax.ShapeDtypeStruct((heads, 3 * tokens, size), BF16),
        rows,
        [pltpu.VMEM(array.shape, BF16) for array in rows] + [pltpu.SemaphoreType.DMA((3,))],
        in_specs=[HBM] * 3,
    )


def spread_call(gathered, feat):
    heads, rows, size = gathered.shape
    maps = (heads, feat, size)
    shape = jax.ShapeDtypeStruct
    return call(
        spread_kernel,
        [shape(maps, F32), shape(maps, F32), shape((1, heads), F32)],
        [gathered],
        [pltpu.VMEM(maps, F32), pltpu.VMEM(maps, F32), pltpu.SemaphoreType.DMA((2,))],
        out_specs=[HBM, HBM, VMEM],
    )


def shards(queries, keys, values, map_query, map_key):
    _, tokens, heads, size = queries.shape
    feat = map_query.shape[-1]
    dp = lax.axis_size("dp")
    ctx = lax.axis_size("ctx")
    token_count = dp * ctx * tokens
    shape = jax.ShapeDtypeStruct
    packed = pack_call(queries, keys, values)
    places = [EXCHANGE.index(block) for block in range(ctx)]
    mine = jnp.asarray(places, jnp.int32)[lax.axis_index("ctx")]
    own_query = lax.dynamic_index_in_dim(jnp.swapaxes(map_query, 1, 2), mine, 0, False)
    own_key = lax.dynamic_index_in_dim(jnp.swapaxes(map_key, 1, 2), mine, 0, False)
    sequence = lax.all_to_all(packed, "ctx", 0, 0, tiled=True, axis_index_groups=[EXCHANGE])
    part = head_call(sequence, own_query, own_key, token_count)
    parts = jnp.broadcast_to(part[None], (dp,) + part.shape)
    parts = lax.all_to_all(parts, "dp", 0, 0, tiled=True, axis_index_groups=[ADD])
    whole = call(add_kernel, shape((ctx,) + part.shape, BF16), [parts])
    gathered = lax.all_to_all(whole, "ctx", 0, 0, tiled=True, axis_index_groups=[GATHER])
    grad_query, grad_key, loss = spread_call(gathered, feat)
    return jnp.swapaxes(grad_query, 1, 2), jnp.swapaxes(grad_key, 1, 2), loss.reshape(heads)


def solution(mesh):
    placed = P("dp", "ctx", "head", None)
    maps = P("head", None, None)
    return jax.shard_map(
        shards,
        mesh=mesh,
        in_specs=(placed, placed, placed, maps, maps),
        out_specs=(maps, maps, P("head")),
        check_vma=False,
    )
```

```python
import functools
import math

import jax
import jax.numpy as jnp
from jax import lax
from jax.experimental import pallas as pl
from jax.experimental.pallas import tpu as pltpu
from jax.sharding import PartitionSpec as P

F32 = jnp.float32
BF16 = jnp.bfloat16
CHUNK = 256
EXCHANGE = [8, 6, 10, 4, 12, 2, 14, 0, 9, 7, 11, 5, 13, 3, 15, 1]
GATHER = [8, 6, 10, 4, 12, 2, 14, 0, 9, 7, 11, 5, 13, 3, 15, 1]
ADD = [6, 1, 4, 7, 5, 3, 0, 2]


def nn(left, right):
    return lax.dot_general(left, right, (((1,), (0,)), ((), ())), preferred_element_type=F32)


def nt(left, right):
    return lax.dot_general(left, right, (((1,), (1,)), ((), ())), preferred_element_type=F32)


def halves(array):
    high = array.astype(BF16)
    return high, (array - high.astype(F32)).astype(BF16)


def wide_nn(left, right):
    rows = left.shape[0]
    both = nn(jnp.concatenate(halves(left), 0), right)
    return both[:rows] + both[rows:]


def sort_rows(groups):
    rows = 256
    span = rows // groups
    shift = span.bit_length() - 1
    to = lax.broadcasted_iota(jnp.int32, (rows, rows), 0)
    source = lax.broadcasted_iota(jnp.int32, (rows, rows), 1)
    wanted = (to & (span - 1)) * groups + (to >> shift)
    return (source == wanted).astype(F32).astype(BF16)


def pack_kernel(q_hbm, k_hbm, v_hbm, out_ref, q_ref, k_ref, v_ref, sems):
    copies = [
        pltpu.make_async_copy(source, target, sems.at[place])
        for place, (source, target) in enumerate(((k_hbm, k_ref), (v_hbm, v_ref), (q_hbm, q_ref)))
    ]
    for copy in copies:
        copy.start()
    heads = out_ref.shape[0]
    tokens = out_ref.shape[1] // 3
    value_heads = k_ref.shape[0] // tokens
    group = heads // value_heads
    order = sort_rows(heads)
    value_order = sort_rows(value_heads)
    for place, ref in enumerate((k_ref, v_ref)):
        span = 256 // value_heads
        copies[place].wait()
        for step in range(tokens // span):
            rows = nn(value_order, ref[step * 256 : (step + 1) * 256, :]).astype(BF16)
            start = (place + 1) * tokens + step * span
            for head in range(heads):
                own = head // group
                out_ref[head, start : start + span, :] = rows[own * span : (own + 1) * span, :]
    span = 256 // heads
    copies[2].wait()
    for step in range(tokens // span):
        rows = nn(order, q_ref[step * 256 : (step + 1) * 256, :]).astype(BF16)
        out_ref[:, step * span : (step + 1) * span, :] = rows.reshape(heads, span, rows.shape[-1])


def feature_halves(inputs, mapping_t):
    logits = nt(mapping_t, inputs)
    positive = jnp.exp(logits - jnp.max(logits, 0, keepdims=True))
    negative = jnp.exp(jnp.min(logits, 0, keepdims=True) - logits)
    positive = positive * (1.0 / jnp.sum(positive, 0, keepdims=True))
    negative = negative * (1.0 / jnp.sum(negative, 0, keepdims=True))
    return positive, negative


def logit_gradient(positive, negative, gradient):
    half = positive.shape[0]
    up = gradient[:half]
    down = gradient[half:]
    up = positive * (up - jnp.sum(up * positive, 0, keepdims=True))
    down = negative * (down - jnp.sum(down * negative, 0, keepdims=True))
    return up - down


def head_kernel(token_count, x_ref, mq_ref, mk_ref, out_ref):
    blocks, rows3, size = x_ref.shape
    tokens = rows3 // 3
    per = CHUNK // tokens
    chunks = range(blocks // per)
    feat = mq_ref.shape[0]
    scale = size**-0.5 * math.log2(math.e)

    def part(which, first, last):
        slots = [EXCHANGE.index(block) for block in range(first * per, last * per)]
        rows = slice(which * tokens, (which + 1) * tokens)
        return jnp.concatenate([x_ref[slot, rows, :] for slot in slots], 0)

    def each(make):
        return [make(c) for c in chunks]

    row = lax.broadcasted_iota(jnp.int32, (CHUNK, CHUNK), 0)
    col = lax.broadcasted_iota(jnp.int32, (CHUNK, CHUNK), 1)
    causal = row >= col
    q = each(lambda c: part(0, c, c + 1))
    k = each(lambda c: part(1, c, c + 1))
    ones = jnp.ones((CHUNK, size), BF16)
    v_wide = each(lambda c: jnp.concatenate([part(2, c, c + 1), ones], 1))
    mq_t = mq_ref[...]
    mk_t = mk_ref[...]

    def feature(c):
        k_halves = feature_halves(k[c], mk_t)
        q_halves = feature_halves(q[c], mq_t)
        q_joined = jnp.concatenate(q_halves, 0)
        phi_kt = jnp.concatenate(k_halves, 0).astype(BF16)
        return k_halves, q_halves, phi_kt, q_joined.astype(BF16), q_joined.T.astype(BF16)

    def block(c):
        last = jnp.where(causal, nt(q[c], k[c]), -jnp.inf)
        if not c:
            return (last,)
        return nt(q[c], part(1, 0, c)), last

    def peak(c):
        return functools.reduce(jnp.maximum, [jnp.max(s, -1, keepdims=True) for s in blocks_of[c]])

    def teacher(c):
        expos = [jnp.exp2((s - peaks[c]) * scale) for s in blocks_of[c]]
        mass = sum(jnp.sum(e, -1, keepdims=True) for e in expos)
        target = nn(expos[-1].astype(BF16), part(2, c, c + 1))
        if c:
            target = target + nn(expos[0].astype(BF16), part(2, 0, c))
        return target * (1.0 / mass)

    def score(c):
        return halves(jnp.where(causal, nn(phi_q[c], phi_kt[c]), 0.0))

    blocks_of = each(block)
    peaks = each(peak)
    target, made = zip(*each(lambda c: (teacher(c), feature(c))))
    k_halves, q_halves, phi_kt, phi_qt, phi_q = zip(*made)
    k_up, k_down = zip(*k_halves)
    q_up, q_down = zip(*q_halves)
    state = [jnp.zeros((2 * feat, 2 * size), F32)]
    for c in chunks[:-1]:
        state.append(state[-1] + nn(phi_kt[c], v_wide[c]))
    state_low = each(lambda c: state[c].astype(BF16))
    scores = each(score)
    summed = each(
        lambda c: nn(scores[c][0], v_wide[c]) + nn(scores[c][1], v_wide[c]) + nn(phi_q[c], state_low[c])
    )
    loss = jnp.zeros((CHUNK, size), F32)
    wide = []
    for c in chunks:
        inverse = 1.0 / summed[c][:, size:]
        student = summed[c][:, :size] * inverse
        residual = student - target[c]
        loss = loss + residual * residual
        gradient = residual * inverse * (2.0 / token_count)
        wide.append(jnp.concatenate([gradient, -gradient * student], 1).astype(BF16))
    suffix = [jnp.zeros((2 * feat, 2 * size), F32)]
    for c in reversed(chunks[1:]):
        suffix.insert(0, suffix[0] + nn(phi_qt[c], wide[c]))
    weights = each(lambda c: halves(jnp.where(causal, nt(wide[c], v_wide[c]), 0.0)))
    q_gradient = each(
        lambda c: nt(phi_kt[c], weights[c][0]) + nt(phi_kt[c], weights[c][1]) + nt(state_low[c], wide[c])
    )
    k_gradient = each(
        lambda c: nn(phi_qt[c], weights[c][0])
        + nn(phi_qt[c], weights[c][1])
        + nt(suffix[c].astype(BF16), v_wide[c])
    )
    query_map = sum(each(lambda c: wide_nn(logit_gradient(q_up[c], q_down[c], q_gradient[c]), q[c])))
    key_map = sum(each(lambda c: wide_nn(logit_gradient(k_up[c], k_down[c], k_gradient[c]), k[c])))
    total = jnp.sum(jnp.sum(loss, 0, keepdims=True), 1, keepdims=True) * (1.0 / token_count)
    out_ref[...] = with_loss(jnp.concatenate([query_map, key_map], 0), total)


def with_loss(maps, total):
    last = maps.shape[0] // 2 - 1
    high = total.astype(BF16).astype(F32)
    row = lax.broadcasted_iota(jnp.int32, maps.shape, 0)
    col = lax.broadcasted_iota(jnp.int32, maps.shape, 1)
    maps = jnp.where((row == last) & (col == 0), high, maps)
    return jnp.where((row == last) & (col == 1), total - high, maps).astype(BF16)


def add_kernel(x_ref, out_ref):
    total = x_ref[0].astype(F32)
    for place in range(1, x_ref.shape[0]):
        total = total + x_ref[place].astype(F32)
    last = total.shape[0] // 2 - 1
    maps = with_loss(total, total[last : last + 1, 0:1] + total[last : last + 1, 1:2])
    for place in range(out_ref.shape[0]):
        out_ref[place] = maps


def spread_kernel(x_ref, query_hbm, key_hbm, loss_ref, query_ref, key_ref, sems):
    heads, feat, size = query_ref.shape
    row = lax.broadcasted_iota(jnp.int32, (feat, size), 0)
    col = lax.broadcasted_iota(jnp.int32, (feat, size), 1)
    swapped = (row == feat - 1) & (col < 2)
    lane = lax.broadcasted_iota(jnp.int32, (1, heads), 1)
    loss = jnp.zeros((1, heads), F32)
    for head in range(heads):
        slot = GATHER.index(EXCHANGE[head])
        maps = x_ref[slot, 0:feat, :].astype(F32)
        rest = jnp.sum(jnp.where(swapped, 0.0, maps), 0, keepdims=True)
        query_ref[head] = jnp.where(swapped, -rest, maps)
        key_ref[head] = x_ref[slot, feat:, :].astype(F32)
        loss = jnp.where(lane == head, maps[feat - 1 :, 0:1] + maps[feat - 1 :, 1:2], loss)
    loss_ref[...] = loss
    copies = [
        pltpu.make_async_copy(source, target, sems.at[place])
        for place, (source, target) in enumerate(((query_ref, query_hbm), (key_ref, key_hbm)))
    ]
    for copy in copies:
        copy.start()
    for copy in copies:
        copy.wait()


VMEM = pl.BlockSpec(memory_space=pltpu.VMEM)


HBM = pl.BlockSpec(memory_space=pltpu.HBM)


def call(kernel, shapes, inputs, scratch=(), limit=32, in_specs=None, out_specs=VMEM):
    return pl.pallas_call(
        kernel,
        out_shape=shapes,
        in_specs=in_specs or [VMEM] * len(inputs),
        out_specs=out_specs,
        scratch_shapes=list(scratch),
        compiler_params=pltpu.CompilerParams(vmem_limit_bytes=limit * 2**20),
    )(*inputs)


def head_call(sequence, own_query, own_key, token_count):
    blocks, rows, size = sequence.shape
    chunks = blocks * rows // 3 // CHUNK
    return call(
        functools.partial(head_kernel, token_count),
        jax.ShapeDtypeStruct((size, size), BF16),
        [sequence, own_query, own_key],
        (),
        48,
    )


def pack_call(queries, keys, values):
    _, tokens, heads, size = queries.shape
    rows = [
        pltpu.with_memory_space_constraint(array.reshape(-1, size), pltpu.HBM)
        for array in (queries, keys, values)
    ]
    return call(
        pack_kernel,
        jax.ShapeDtypeStruct((heads, 3 * tokens, size), BF16),
        rows,
        [pltpu.VMEM(array.shape, BF16) for array in rows] + [pltpu.SemaphoreType.DMA((3,))],
        in_specs=[HBM] * 3,
    )


def spread_call(gathered, feat):
    heads, rows, size = gathered.shape
    maps = (heads, feat, size)
    shape = jax.ShapeDtypeStruct
    return call(
        spread_kernel,
        [shape(maps, F32), shape(maps, F32), shape((1, heads), F32)],
        [gathered],
        [pltpu.VMEM(maps, F32), pltpu.VMEM(maps, F32), pltpu.SemaphoreType.DMA((2,))],
        out_specs=[HBM, HBM, VMEM],
    )


def shards(queries, keys, values, map_query, map_key):
    _, tokens, heads, size = queries.shape
    feat = map_query.shape[-1]
    dp = lax.axis_size("dp")
    ctx = lax.axis_size("ctx")
    token_count = dp * ctx * tokens
    shape = jax.ShapeDtypeStruct
    packed = pack_call(queries, keys, values)
    places = [EXCHANGE.index(block) for block in range(ctx)]
    mine = jnp.asarray(places, jnp.int32)[lax.axis_index("ctx")]
    own_query = lax.dynamic_index_in_dim(jnp.swapaxes(map_query, 1, 2), mine, 0, False)
    own_key = lax.dynamic_index_in_dim(jnp.swapaxes(map_key, 1, 2), mine, 0, False)
    sequence = lax.all_to_all(packed, "ctx", 0, 0, tiled=True, axis_index_groups=[EXCHANGE])
    part = head_call(sequence, own_query, own_key, token_count)
    parts = jnp.broadcast_to(part[None], (dp,) + part.shape)
    parts = lax.all_to_all(parts, "dp", 0, 0, tiled=True, axis_index_groups=[ADD])
    whole = call(add_kernel, shape((ctx,) + part.shape, BF16), [parts])
    gathered = lax.all_to_all(whole, "ctx", 0, 0, tiled=True, axis_index_groups=[GATHER])
    grad_query, grad_key, loss = spread_call(gathered, feat)
    return jnp.swapaxes(grad_query, 1, 2), jnp.swapaxes(grad_key, 1, 2), loss.reshape(heads)


def solution(mesh):
    placed = P("dp", "ctx", "head", None)
    maps = P("head", None, None)
    return jax.shard_map(
        shards,
        mesh=mesh,
        in_specs=(placed, placed, placed, maps, maps),
        out_specs=(maps, maps, P("head")),
        check_vma=False,
    )
```
